32 devices in a mesh: freq: 8 (over z, y), blk: 4 (over x, core).
Axes of the slice: x: 2, y: 2, z: 4, core: 2. Of those that a mesh axis runs over, the one named last changes fastest.
Arguments:
- samples: int32 [1024, 417792], P(('blk', 'freq')), may hold values from -8 to 7
Outputs:
- visibilities: bfloat16 [2, 96, 1024, 1024], P(None, 'freq', 'blk')
The draws below stay inside these ranges and needn't reach their ends.
All inputs are finite; a program needn't handle non-finite values.
Results may differ from the reference program's by a relative error of at most 0.0079.
Values may be sent and summed in bfloat16 or wider, within the bound.
No kernel may reach another device: no remote copies, remote signals or barrier semaphores. Data moves between devices by JAX's collectives and lax.ppermute only.
A program may use at most 320 MiB of HBM per device.

```python
import math
import jax
import jax.numpy as jnp
from jax import lax

A = 1024
FRAME = 8192
TAPS = 4
NSPEC = 48
NFRAMES = 51
SAMPLES = 417792
CHANNELS = 96


def plant(array, stream_key, smallest, high):
    spot = [jax.random.randint(jax.random.fold_in(stream_key, axis), (), 0, length) for axis, length in enumerate(array.shape)]
    widest = array.shape.index(max(array.shape))
    beside = spot[:widest] + [(spot[widest] + 1) % array.shape[widest]] + spot[widest + 1:]
    return array.at[tuple(spot)].set(smallest).at[tuple(beside)].set(high)


def setup_inputs(seed: int = 0) -> dict:
    key_of = jax.random.split(jax.random.key(seed), 2)
    samples = plant(jax.random.randint(key_of[0], (A, SAMPLES), -8, 8), jax.random.fold_in(key_of[0], 1), -8, 7).astype(jnp.int32)
    return {"samples": samples}


def make_window(frame, taps):
    length = taps * frame
    moment = jnp.arange(length, dtype=jnp.float32)
    offset = (moment + 0.5 - length / 2.0) / frame
    taper = 0.5 - 0.5 * jnp.cos(2.0 * math.pi * (moment + 0.5) / length)
    return (jnp.sinc(offset) * taper).reshape(taps, frame)

def make_table(frame, channels):
    index = jnp.arange(frame, dtype=jnp.int32)[:, None]
    column = jnp.arange(channels, dtype=jnp.int32)[None, :] + 1
    phase = (index * column % frame).astype(jnp.float32) * (2.0 * math.pi / frame)
    factor = 1.0 / math.sqrt(21.25 * frame)
    both = jnp.concatenate([jnp.cos(phase) * factor, -jnp.sin(phase) * factor], axis=1)
    return both.astype(jnp.bfloat16)

def reference(samples):
    window = make_window(FRAME, TAPS)
    table = make_table(FRAME, CHANNELS).astype(jnp.float32)
    group = 64 if A % 64 == 0 else A
    grouped = samples.reshape(A // group, group, SAMPLES)

    def one_group(block):
        frames = block.reshape(group, NFRAMES, FRAME).astype(jnp.float32)
        filtered = frames[:, 0:NSPEC, :] * window[0]
        for k in range(1, TAPS):
            filtered = filtered + frames[:, k:k + NSPEC, :] * window[k]
        filtered = filtered.astype(jnp.bfloat16).astype(jnp.float32)
        spec = jnp.einsum('fc,asf->csa', table, filtered)
        return spec.astype(jnp.bfloat16)
    pieces = lax.map(one_group, grouped)
    spectra = jnp.transpose(pieces, (1, 2, 0, 3)).reshape(2, CHANNELS, NSPEC, A)
    spectra = spectra.astype(jnp.float32)

    def one_channel(index):
        real_in = spectra[0, index]
        imag_in = spectra[1, index]
        real_out = jnp.einsum('sa,sb->ab', real_in, real_in) + jnp.einsum('sa,sb->ab', imag_in, imag_in)
        imag_out = jnp.einsum('sa,sb->ab', imag_in, real_in) - jnp.einsum('sa,sb->ab', real_in, imag_in)
        return (jnp.stack([real_out, imag_out]) / NSPEC).astype(jnp.bfloat16)
    result = lax.map(one_channel, jnp.arange(CHANNELS, dtype=jnp.int32))
    return jnp.transpose(result, (1, 0, 2, 3))
```

```python
import math

import jax
import jax.numpy as jnp
import ml_dtypes
import numpy as np
from jax import lax
from jax.experimental import pallas as pl
from jax.experimental.pallas import tpu as pltpu
from jax.sharding import PartitionSpec as P

FRAME = 8192
TAPS = 4
CH_DEV = 12
NSPEC = 48
LANES = 128
PAIR = 2 * NSPEC
BLOCK = 1024
VMEM_LIMIT = 48 * 1024 * 1024


def make_window(frame, taps):
    length = taps * frame
    moment = np.arange(length, dtype=np.float64)
    offset = (moment + 0.5 - length / 2.0) / frame
    taper = 0.5 - 0.5 * np.cos(2.0 * math.pi * (moment + 0.5) / length)
    return (np.sinc(offset) * taper).astype(np.float32).reshape(taps, frame)


def make_table(frame, channels, width):
    index = np.arange(frame, dtype=np.int64)[:, None]
    column = np.arange(channels, dtype=np.int64)[None, :] + 1
    phase = (index * column % frame).astype(np.float64) * (2.0 * math.pi / frame)
    factor = 1.0 / math.sqrt(21.25 * frame)
    table = np.zeros((frame, 2 * width), np.float32)
    table[:, :channels] = np.cos(phase) * factor
    table[:, width : width + channels] = -np.sin(phase) * factor
    return table.astype(ml_dtypes.bfloat16)


def filterbank_kernel(rows, channels, width, x_ref, w_ref, t_ref, o_ref, filt, acc, turned):
    step = pl.program_id(0)
    groups = rows // 8
    tiles = BLOCK // LANES

    def one_tile(tile, carry):
        lanes = pl.ds(pl.multiple_of(tile * LANES, LANES), LANES)
        taps = [w_ref[pl.ds(k, 1), lanes] for k in range(TAPS)]
        held = [[x_ref[g, f, tile].astype(jnp.float32) for f in range(TAPS - 1)] for g in range(groups)]
        pending = []
        for s in range(NSPEC):
            for g in range(groups):
                held[g].append(x_ref[g, s + TAPS - 1, tile].astype(jnp.float32))
                total = held[g][0] * taps[0]
                for k in range(1, TAPS):
                    total = total + held[g][k] * taps[k]
                held[g].pop(0)
                pending.append(total)
                if len(pending) == 2:
                    row = (s * groups + g - 1) * 8
                    filt[pl.ds(row, 16), lanes] = jnp.concatenate(pending, axis=0).astype(jnp.bfloat16)
                    pending = []
        return carry

    lax.fori_loop(0, tiles, one_tile, 0)
    part = jnp.dot(filt[...], t_ref[...], preferred_element_type=jnp.float32)

    halves = [part[:, h * LANES : (h + 1) * LANES] for h in range(2 * width // LANES)]

    @pl.when(step == 0)
    def _():
        for h, half in enumerate(halves):
            acc[h] = half

    @pl.when(step > 0)
    def _():
        for h, half in enumerate(halves):
            acc[h] += half

    @pl.when(step == pl.num_programs(0) - 1)
    def _():
        for c in range(width // LANES):
            count = min(LANES, channels - c * LANES)
            for a in range(rows):
                both = jnp.concatenate(
                    [
                        acc[p * (width // LANES) + c, pl.ds(a, NSPEC, stride=rows), :]
                        for p in range(2)
                    ],
                    axis=0,
                )
                turned[pl.ds(c * LANES * rows + a, count, stride=rows), pl.ds(0, PAIR)] = both.T[:count]
        lane = lax.broadcasted_iota(jnp.int32, (rows, LANES), 1)
        for q in range(channels // 4):
            one = [turned[pl.ds((4 * q + i) * rows, rows), :] for i in range(4)]
            one = [one[0]] + [pltpu.roll(one[i], LANES - 32 * i, 1) for i in range(1, 4)]
            out = [jnp.where(lane < LANES - 32 * (i + 1), one[i], one[i + 1]) for i in range(3)]
            out = jnp.concatenate(out, axis=1).astype(jnp.bfloat16)
            dest, place = q // (CH_DEV // 4), q % (CH_DEV // 4)
            o_ref[dest, :, pl.ds(place * 384, 384)] = out


def filterbank(samples, window, table, piece, rows, shards):
    antenna_groups, frames, steps, _, _ = samples.shape
    groups = rows // 8
    channels = CH_DEV * shards
    width = table.shape[1] // 2
    tiles = BLOCK // LANES
    spec_rows = NSPEC * rows
    flops = 2 * spec_rows * FRAME * 2 * width
    return pl.pallas_call(
        lambda *refs: filterbank_kernel(rows, channels, width, *refs),
        grid=(FRAME // BLOCK,),
        in_specs=[
            pl.BlockSpec((groups, frames, tiles, 8, LANES), lambda i: (piece, 0, i, 0, 0)),
            pl.BlockSpec((TAPS, BLOCK), lambda i: (0, i)),
            pl.BlockSpec((BLOCK, 2 * width), lambda i: (i, 0)),
        ],
        out_specs=pl.BlockSpec((shards, rows, CH_DEV * PAIR), lambda i: (0, 0, 0)),
        out_shape=jax.ShapeDtypeStruct((shards, rows, CH_DEV * PAIR), jnp.bfloat16),
        scratch_shapes=[
            pltpu.VMEM((spec_rows, BLOCK), jnp.bfloat16),
            pltpu.VMEM((2 * width // LANES, spec_rows, LANES), jnp.float32),
            pltpu.VMEM((channels * rows, LANES), jnp.float32),
        ],
        compiler_params=pltpu.CompilerParams(vmem_limit_bytes=VMEM_LIMIT),
        cost_estimate=pl.CostEstimate(
            flops=flops, bytes_accessed=4 * rows * frames * FRAME, transcendentals=0
        ),
        name="filterbank",
    )(samples, window, table)


def correlate_kernel(pieces, rows, shards, blocks, *refs):
    place, own = refs[0], refs[1 : 1 + pieces]
    cols = refs[1 + pieces : 1 + pieces + blocks * pieces]
    out = refs[-1]
    step = pl.program_id(0)
    local = shards * pieces * rows
    base = pl.multiple_of((step // 2) * 384 + (step % 2) * LANES, LANES)
    window = pl.ds(base, 256)

    def gather(parts):
        loaded = [part[:, :, window] for part in parts]
        return jnp.stack(loaded, axis=1).reshape(local, 256)

    mine = gather(own).astype(jnp.float32)
    lane = lax.broadcasted_iota(jnp.int32, (local, 256), 1)
    ahead, behind = pltpu.roll(mine, 256 - NSPEC, 1), pltpu.roll(mine, NSPEC, 1)
    left = []
    for i in range(2):
        start = lane - ((step % 2) * 64 + i * PAIR)
        real = (start >= 0) & (start < NSPEC)
        imag = (start >= NSPEC) & (start < PAIR)
        left.append(jnp.where(real | imag, mine, 0.0).astype(jnp.bfloat16))
        left.append(jnp.where(real, ahead, jnp.where(imag, -behind, 0.0)).astype(jnp.bfloat16))
    left = jnp.concatenate(left, axis=0)
    for n in range(blocks):
        right = gather(cols[n * pieces : (n + 1) * pieces])
        term = lax.dot_general(left, right, (((1,), (1,)), ((), ())), preferred_element_type=jnp.float32)
        term = (term * (1.0 / NSPEC)).astype(jnp.bfloat16)
        at = pl.ds(pl.multiple_of(place[n] * local, LANES), local)
        for i in range(2):
            for p in range(2):
                k = 2 * i + p
                out[p, i, :, at] = term[k * local : (k + 1) * local]


def correlate(place, own, cols, width):
    pieces = len(own)
    blocks = len(cols) // pieces
    shards, rows, depth = own[0].shape
    local = shards * pieces * rows
    whole = pl.BlockSpec((shards, rows, depth), lambda i, *_: (0, 0, 0))
    return pl.pallas_call(
        lambda *refs: correlate_kernel(pieces, rows, shards, blocks, *refs),
        grid_spec=pltpu.PrefetchScalarGridSpec(
            num_scalar_prefetch=1,
            grid=(CH_DEV // 2,),
            in_specs=[whole] * (pieces + len(cols)),
            out_specs=pl.BlockSpec((2, 2, local, width), lambda i, *_: (0, i, 0, 0)),
        ),
        out_shape=jax.ShapeDtypeStruct((2, CH_DEV, local, width), jnp.bfloat16),
        compiler_params=pltpu.CompilerParams(vmem_limit_bytes=VMEM_LIMIT),
        cost_estimate=pl.CostEstimate(
            flops=2 * 2 * CH_DEV * local * local * blocks * 256,
            bytes_accessed=2 * 2 * CH_DEV * local * local * blocks,
            transcendentals=0,
        ),
        name="correlate",
    )(place, *own, *cols)


def exchange(value, axis, distance):
    count = lax.axis_size(axis)
    return lax.ppermute(value, axis, [(i, i ^ distance) for i in range(count)])


def per_device(samples):
    antennas, length = samples.shape
    shards = lax.axis_size("freq")
    blocks = lax.axis_size("blk")
    channels = CH_DEV * shards
    frames = length // FRAME
    width = -(-channels // LANES) * LANES
    rows = 16 if antennas % 16 == 0 else 8
    pieces = antennas // rows
    window = jnp.asarray(make_window(FRAME, TAPS))
    table = jnp.asarray(make_table(FRAME, channels, width))
    tiled = samples.reshape(antennas // 8, 8, length // LANES, LANES).transpose(0, 2, 1, 3)
    tiled = tiled.reshape(antennas // 8, frames, FRAME // LANES, 8, LANES)
    held = []
    for piece in range(pieces):
        spectra = filterbank(tiled, window, table, piece, rows, shards)
        turned = lax.all_to_all(spectra, "freq", split_axis=0, concat_axis=0, tiled=True)
        far = exchange(turned, "blk", 2)
        near = exchange(turned, "blk", 1)
        last = exchange(far, "blk", 1)
        held.append([turned, near, far, last])
    me = lax.axis_index("blk")
    place = jnp.stack([me ^ n for n in range(blocks)]).astype(jnp.int32)
    own = [held[p][0] for p in range(pieces)]
    cols = [held[p][n] for n in range(blocks) for p in range(pieces)]
    return correlate(place, own, cols, antennas * shards * blocks)


def solution(mesh):
    in_specs = (P(("blk", "freq"), None),)
    out_specs = P(None, "freq", "blk", None)
    return jax.shard_map(
        per_device, mesh=mesh, in_specs=in_specs, out_specs=out_specs, check_vma=False
    )
```

```python
import math

import jax
import jax.numpy as jnp
import ml_dtypes
import numpy as np
from jax import lax
from jax.experimental import pallas as pl
from jax.experimental.pallas import tpu as pltpu
from jax.sharding import PartitionSpec as P

FRAME = 8192
TAPS = 4
CH_DEV = 12
NSPEC = 48
LANES = 128
PAIR = 2 * NSPEC
BLOCK = 2048
PARTS = ((0, 4), (4, 4), (8, 8), (16, 16), (32, 16), (48, 16))
FILTER_VMEM = 60 * 1024 * 1024
CORRELATE_VMEM = 32 * 1024 * 1024


def make_window(frame, taps):
    length = taps * frame
    moment = np.arange(length, dtype=np.float64)
    offset = (moment + 0.5 - length / 2.0) / frame
    taper = 0.5 - 0.5 * np.cos(2.0 * math.pi * (moment + 0.5) / length)
    return (np.sinc(offset) * taper).astype(np.float32).reshape(taps, frame)


def make_table(frame, channels, width):
    index = np.arange(frame, dtype=np.int64)[:, None]
    column = np.arange(channels, dtype=np.int64)[None, :] + 1
    phase = (index * column % frame).astype(np.float64) * (2.0 * math.pi / frame)
    factor = 1.0 / math.sqrt(21.25 * frame)
    table = np.zeros((frame, 2 * width), np.float32)
    table[:, :channels] = np.cos(phase) * factor
    table[:, width : width + channels] = -np.sin(phase) * factor
    return table.astype(ml_dtypes.bfloat16)


def filterbank_kernel(piece, rows, channels, width, x_hbm, w_ref, t_hbm, o_ref, x_ref, t_ref, filt, acc, turned, x_sem, t_sem):
    groups = rows // 8
    spec_rows = NSPEC * rows
    tiles = BLOCK // LANES

    def x_copy(n):
        first, count = PARTS[n]
        where = pl.ds(first, count)
        return pltpu.make_async_copy(
            x_hbm.at[pl.ds(piece * groups, groups), :, where], x_ref.at[:, :, where], x_sem.at[n]
        )

    def t_copy(b):
        return pltpu.make_async_copy(t_hbm.at[pl.ds(b * BLOCK, BLOCK)], t_ref.at[b], t_sem.at[b])

    for n, (first, count) in enumerate(PARTS):
        x_copy(n).start()
        if (first + count) % tiles == 0:
            t_copy(first // tiles).start()

    def one_tile(tile, slot):
        taps = [w_ref[pl.ds(k, 1), pl.ds(pl.multiple_of(tile * LANES, LANES), LANES)] for k in range(TAPS)]
        held = [[x_ref[g, f, tile].astype(jnp.float32) for f in range(TAPS - 1)] for g in range(groups)]
        ready = []
        for s in range(NSPEC):
            for g in range(groups):
                held[g].append(x_ref[g, s + TAPS - 1, tile].astype(jnp.float32))
                total = held[g][0] * taps[0]
                for k in range(1, TAPS):
                    total = total + held[g][k] * taps[k]
                held[g].pop(0)
                ready.append(total)
                if len(ready) == 2:
                    row = (s * groups + g - 1) * 8
                    filt[slot, pl.ds(row, 16), :] = jnp.concatenate(ready, axis=0).astype(jnp.bfloat16)
                    ready = []

    for n, (first, count) in enumerate(PARTS):
        x_copy(n).wait()
        base = first % tiles

        def step(i, carry, first=first, base=base):
            one_tile(first + i, base + i)
            return carry

        lax.fori_loop(0, count, step, 0)
        if (first + count) % tiles:
            continue
        b = first // tiles
        t_copy(b).wait()
        left = jnp.concatenate([filt[k] for k in range(tiles)], axis=1)
        for m in range(2):
            span = slice(m * spec_rows // 2, (m + 1) * spec_rows // 2)
            part = jnp.dot(left[span], t_ref[b], preferred_element_type=jnp.float32)
            for h in range(2 * width // LANES):
                half = part[:, h * LANES : (h + 1) * LANES]
                if b == 0:
                    acc[h, span] = half
                else:
                    acc[h, span] += half

    for c in range(width // LANES):
        count = min(LANES, channels - c * LANES)
        for a in range(rows):
            both = jnp.concatenate(
                [acc[p * (width // LANES) + c, pl.ds(a, NSPEC, stride=rows), :] for p in range(2)], axis=0
            )
            turned[pl.ds(c * LANES * rows + a, count, stride=rows), pl.ds(0, PAIR)] = both.T[:count]
    lane = lax.broadcasted_iota(jnp.int32, (rows, LANES), 1)
    for q in range(channels // 4):
        one = [turned[pl.ds((4 * q + i) * rows, rows), :] for i in range(4)]
        one = [one[0]] + [pltpu.roll(one[i], LANES - 32 * i, 1) for i in range(1, 4)]
        dest, place = q // (CH_DEV // 4), q % (CH_DEV // 4)
        for i in range(3):
            tile = jnp.where(lane < LANES - 32 * (i + 1), one[i], one[i + 1])
            o_ref[dest, place * 3 + i] = tile.astype(jnp.bfloat16)


def filterbank(samples, window, table, piece, rows, shards):
    antenna_groups, frames, _, _, _ = samples.shape
    groups = rows // 8
    channels = CH_DEV * shards
    width = table.shape[1] // 2
    spec_rows = NSPEC * rows
    shape = (shards, CH_DEV * PAIR // LANES, rows, LANES)
    return pl.pallas_call(
        lambda *refs: filterbank_kernel(piece, rows, channels, width, *refs),
        in_specs=[
            pl.BlockSpec(memory_space=pl.ANY),
            pl.BlockSpec(memory_space=pltpu.VMEM),
            pl.BlockSpec(memory_space=pl.ANY),
        ],
        out_specs=pl.BlockSpec(memory_space=pltpu.VMEM),
        out_shape=jax.ShapeDtypeStruct(shape, jnp.bfloat16),
        scratch_shapes=[
            pltpu.VMEM((groups, frames, FRAME // LANES, 8, LANES), jnp.int32),
            pltpu.VMEM((FRAME // BLOCK, BLOCK, 2 * width), jnp.bfloat16),
            pltpu.VMEM((BLOCK // LANES, spec_rows, LANES), jnp.bfloat16),
            pltpu.VMEM((2 * width // LANES, spec_rows, LANES), jnp.float32),
            pltpu.VMEM((channels * rows, LANES), jnp.float32),
            pltpu.SemaphoreType.DMA((len(PARTS),)),
            pltpu.SemaphoreType.DMA((FRAME // BLOCK,)),
        ],
        compiler_params=pltpu.CompilerParams(vmem_limit_bytes=FILTER_VMEM),
        cost_estimate=pl.CostEstimate(
            flops=2 * spec_rows * FRAME * 2 * width, bytes_accessed=4 * rows * frames * FRAME, transcendentals=0
        ),
        name="filterbank",
    )(samples, window, table)


def correlate_kernel(pieces, blocks, *refs):
    place, own = refs[0], refs[1 : 1 + pieces]
    cols = refs[1 + pieces : 1 + pieces + blocks * pieces]
    out = refs[-1]
    shards, _, rows, _ = own[0].shape
    local = shards * pieces * rows
    lane = lax.broadcasted_iota(jnp.int32, (local, 256), 1)

    def gather(parts):
        return [jnp.stack([part[:, u] for part in parts], axis=1).reshape(local, LANES) for u in range(3)]

    mine = gather(own)
    rights = [gather(cols[n * pieces : (n + 1) * pieces]) for n in range(blocks)]
    for w in range(2):
        held = jnp.concatenate(mine[w : w + 2], axis=1).astype(jnp.float32)
        ahead, behind = pltpu.roll(held, 256 - NSPEC, 1), pltpu.roll(held, NSPEC, 1)
        left = []
        for i in range(2):
            start = w * 64 + i * PAIR
            real = (lane >= start) & (lane < start + NSPEC)
            imag = (lane >= start + NSPEC) & (lane < start + PAIR)
            left.append(jnp.where(real | imag, held, 0.0).astype(jnp.bfloat16))
            left.append(jnp.where(real, ahead, jnp.where(imag, -behind, 0.0)).astype(jnp.bfloat16))
        left = jnp.concatenate(left, axis=0)
        for n in range(blocks):
            right = jnp.concatenate(rights[n][w : w + 2], axis=1)
            term = lax.dot_general(left, right, (((1,), (1,)), ((), ())), preferred_element_type=jnp.float32)
            term = (term * (1.0 / NSPEC)).astype(jnp.bfloat16)
            at = pl.ds(pl.multiple_of(place[1 + n] * local, LANES), local)
            for i in range(2):
                for p in range(2):
                    k = 2 * i + p
                    out[p, 2 * w + i, :, at] = term[k * local : (k + 1) * local]


def correlate(place, own, cols, parts, before=None):
    pieces = len(own)
    blocks = len(cols) // pieces
    shards, tiles, rows, _ = own[0].shape
    local = shards * pieces * rows
    width = local * blocks
    three = pl.BlockSpec((shards, 3, rows, LANES), lambda i, place: (0, i, 0, 0))
    extra = [] if before is None else [before]
    operands = [place, *own, *cols, *extra]

    def body(*refs):
        return correlate_kernel(pieces, blocks, *refs[: 1 + pieces + len(cols)], refs[-1])

    return pl.pallas_call(
        body,
        grid_spec=pltpu.PrefetchScalarGridSpec(
            num_scalar_prefetch=1,
            grid=(CH_DEV // 4,),
            in_specs=[three] * (pieces + len(cols)) + [pl.BlockSpec(memory_space=pl.ANY)] * len(extra),
            out_specs=pl.BlockSpec((2, 4, local, width), lambda i, place: (0, i, 0, place[0])),
        ),
        out_shape=jax.ShapeDtypeStruct((2, CH_DEV, local, width * parts), jnp.bfloat16),
        input_output_aliases={len(operands) - 1: 0} if extra else {},
        compiler_params=pltpu.CompilerParams(vmem_limit_bytes=CORRELATE_VMEM),
        cost_estimate=pl.CostEstimate(
            flops=2 * 2 * CH_DEV * local * width * 256, bytes_accessed=2 * 2 * CH_DEV * local * width, transcendentals=0
        ),
        name="correlate",
    )(*operands)


def exchange(value, axis, distance):
    count = lax.axis_size(axis)
    return lax.ppermute(value, axis, [(i, i ^ distance) for i in range(count)])


def per_device(samples):
    antennas, length = samples.shape
    shards = lax.axis_size("freq")
    blocks = lax.axis_size("blk")
    channels = CH_DEV * shards
    frames = length // FRAME
    width = -(-channels // LANES) * LANES
    rows = 16 if antennas % 16 == 0 else 8
    pieces = antennas // rows
    window = jnp.asarray(make_window(FRAME, TAPS))
    table = jnp.asarray(make_table(FRAME, channels, width))
    tiled = samples.reshape(antennas // 8, 8, length // LANES, LANES).transpose(0, 2, 1, 3)
    tiled = tiled.reshape(antennas // 8, frames, FRAME // LANES, 8, LANES)
    own, near, far = [], [], []
    for piece in range(pieces):
        spectra = filterbank(tiled, window, table, piece, rows, shards)
        own.append(lax.all_to_all(spectra, "freq", split_axis=0, concat_axis=0, tiled=True))
        far.append(exchange(own[piece], "blk", 2))
        near.append(exchange(own[piece], "blk", 1))
    me = lax.axis_index("blk")

    def place(n):
        return jnp.stack([(me ^ n) >> 1, me & 1, (me & 1) ^ 1]).astype(jnp.int32)

    last = [exchange(value, "blk", 1) for value in far[:-1]]
    own, near, far[:-1], last = lax.optimization_barrier((own, near, far[:-1], last))
    result = correlate(place(0), own, own + near, blocks // 2)
    result, far[-1] = lax.optimization_barrier((result, far[-1]))
    last.append(exchange(far[-1], "blk", 1))
    return correlate(place(2), own, far + last, blocks // 2, result)


def solution(mesh):
    in_specs = (P(("blk", "freq"), None),)
    out_specs = P(None, "freq", "blk", None)
    return jax.shard_map(
        per_device, mesh=mesh, in_specs=in_specs, out_specs=out_specs, check_vma=False
    )
```

```python
import math

import jax
import jax.numpy as jnp
import ml_dtypes
import numpy as np
from jax import lax
from jax.experimental import pallas as pl
from jax.experimental.pallas import tpu as pltpu
from jax.sharding import PartitionSpec as P

FRAME = 8192
TAPS = 4
CH_DEV = 12
NSPEC = 48
LANES = 128
PAIR = 2 * NSPEC
BLOCK = 2048
PARTS = ((0, 4), (4, 4), (8, 8), (16, 16), (32, 16), (48, 8), (56, 8))
FILTER_VMEM = 60 * 1024 * 1024
CORRELATE_VMEM = 32 * 1024 * 1024


def make_window(frame, taps):
    length = taps * frame
    moment = np.arange(length, dtype=np.float64)
    offset = (moment + 0.5 - length / 2.0) / frame
    taper = 0.5 - 0.5 * np.cos(2.0 * math.pi * (moment + 0.5) / length)
    w = (np.sinc(offset) * taper).astype(np.float32).reshape(taps, frame // LANES, 1, LANES)
    return np.ascontiguousarray(np.broadcast_to(w, (taps, frame // LANES, 8, LANES)))


def make_table(frame, channels, width):
    index = np.arange(frame, dtype=np.int64)[:, None]
    column = np.arange(channels, dtype=np.int64)[None, :] + 1
    phase = (index * column % frame).astype(np.float64) * (2.0 * math.pi / frame)
    factor = 1.0 / math.sqrt(21.25 * frame)
    table = np.zeros((frame, 2 * width), np.float32)
    table[:, :channels] = np.cos(phase) * factor
    table[:, width : width + channels] = -np.sin(phase) * factor
    return table.astype(ml_dtypes.bfloat16)


def filterbank_kernel(piece, rows, channels, width, x_hbm, w_hbm, t_hbm, o_hbm, x_ref, w_ref, t_ref, filt, acc, turned, o_ref, x_sem, w_sem, t_sem, o_sem):
    groups = rows // 8
    spec_rows = NSPEC * rows
    tiles = BLOCK // LANES

    def x_copy(n):
        first, count = PARTS[n]
        where = pl.ds(first, count)
        return pltpu.make_async_copy(
            x_hbm.at[pl.ds(piece * groups, groups), :, where], x_ref.at[:, :, where], x_sem.at[n]
        )

    def t_copy(b):
        return pltpu.make_async_copy(t_hbm.at[pl.ds(b * BLOCK, BLOCK)], t_ref.at[b], t_sem.at[b])

    def o_copy(dest):
        return pltpu.make_async_copy(o_ref.at[dest], o_hbm.at[dest], o_sem.at[dest])

    def w_copy(n):
        where = pl.ds(*PARTS[n])
        return pltpu.make_async_copy(w_hbm.at[:, where], w_ref.at[:, where], w_sem.at[n])

    for n, (first, count) in enumerate(PARTS):
        x_copy(n).start()
        w_copy(n).start()
        if (first + count) % tiles == 0:
            t_copy(first // tiles).start()

    def one_tile(tile, slot):
        taps = [w_ref[k, tile] for k in range(TAPS)]
        held = [[x_ref[g, f, tile].astype(jnp.float32) for f in range(TAPS - 1)] for g in range(groups)]
        ready = []
        for s in range(NSPEC):
            for g in range(groups):
                held[g].append(x_ref[g, s + TAPS - 1, tile].astype(jnp.float32))
                total = held[g][0] * taps[0]
                for k in range(1, TAPS):
                    total = total + held[g][k] * taps[k]
                held[g].pop(0)
                ready.append(total)
                if len(ready) == 2:
                    row = (s * groups + g - 1) * 8
                    filt[slot, pl.ds(row, 16), :] = jnp.concatenate(ready, axis=0).astype(jnp.bfloat16)
                    ready = []

    for n, (first, count) in enumerate(PARTS):
        x_copy(n).wait()
        w_copy(n).wait()
        base = first % tiles

        def step(i, carry, first=first, base=base):
            one_tile(first + 2 * i, base + 2 * i)
            one_tile(first + 2 * i + 1, base + 2 * i + 1)
            return carry

        lax.fori_loop(0, count // 2, step, 0)
        if (first + count) % tiles:
            continue
        b = first // tiles
        t_copy(b).wait()
        left = jnp.concatenate([filt[k] for k in range(tiles)], axis=1)
        for m in range(2):
            span = slice(m * spec_rows // 2, (m + 1) * spec_rows // 2)
            part = jnp.dot(left[span], t_ref[b], preferred_element_type=jnp.float32)
            for h in range(2 * width // LANES):
                half = part[:, h * LANES : (h + 1) * LANES]
                if b == 0:
                    acc[h, span] = half
                else:
                    acc[h, span] += half

    for c in range(width // LANES):
        count = min(LANES, channels - c * LANES)
        for a in range(rows):
            both = jnp.concatenate(
                [acc[p * (width // LANES) + c, pl.ds(a, NSPEC, stride=rows), :] for p in range(2)], axis=0
            )
            turned[pl.ds(c * LANES * rows + a, count, stride=rows), pl.ds(0, PAIR)] = both.T[:count]
    lane = lax.broadcasted_iota(jnp.int32, (rows, LANES), 1)
    for q in range(channels // 4):
        one = [turned[pl.ds((4 * q + i) * rows, rows), :] for i in range(4)]
        one = [one[0]] + [pltpu.roll(one[i], LANES - 32 * i, 1) for i in range(1, 4)]
        dest, place = q // (CH_DEV // 4), q % (CH_DEV // 4)
        for i in range(3):
            tile = jnp.where(lane < LANES - 32 * (i + 1), one[i], one[i + 1])
            o_ref[dest, place * 3 + i] = tile.astype(jnp.bfloat16)
        if place == CH_DEV // 4 - 1:
            o_copy(dest).start()
    for dest in range(channels // CH_DEV):
        o_copy(dest).wait()


def filterbank(samples, window, table, piece, rows, shards):
    antenna_groups, frames, _, _, _ = samples.shape
    groups = rows // 8
    channels = CH_DEV * shards
    width = table.shape[1] // 2
    spec_rows = NSPEC * rows
    shape = (shards, CH_DEV * PAIR // LANES, rows, LANES)
    return pl.pallas_call(
        lambda *refs: filterbank_kernel(piece, rows, channels, width, *refs),
        in_specs=[
            pl.BlockSpec(memory_space=pl.ANY),
            pl.BlockSpec(memory_space=pl.ANY),
            pl.BlockSpec(memory_space=pl.ANY),
        ],
        out_specs=pl.BlockSpec(memory_space=pl.ANY),
        out_shape=jax.ShapeDtypeStruct(shape, jnp.bfloat16),
        scratch_shapes=[
            pltpu.VMEM((groups, frames, FRAME // LANES, 8, LANES), jnp.int32),
            pltpu.VMEM((TAPS, FRAME // LANES, 8, LANES), jnp.float32),
            pltpu.VMEM((FRAME // BLOCK, BLOCK, 2 * width), jnp.bfloat16),
            pltpu.VMEM((BLOCK // LANES, spec_rows, LANES), jnp.bfloat16),
            pltpu.VMEM((2 * width // LANES, spec_rows, LANES), jnp.float32),
            pltpu.VMEM((channels * rows, LANES), jnp.float32),
            pltpu.VMEM(shape, jnp.bfloat16),
            pltpu.SemaphoreType.DMA((len(PARTS),)),
            pltpu.SemaphoreType.DMA((len(PARTS),)),
            pltpu.SemaphoreType.DMA((FRAME // BLOCK,)),
            pltpu.SemaphoreType.DMA((shards,)),
        ],
        compiler_params=pltpu.CompilerParams(vmem_limit_bytes=FILTER_VMEM),
        cost_estimate=pl.CostEstimate(
            flops=2 * spec_rows * FRAME * 2 * width, bytes_accessed=4 * rows * frames * FRAME, transcendentals=0
        ),
        name="filterbank",
    )(samples, window, table)


def correlate_kernel(pieces, blocks, *refs):
    place, own = refs[0], refs[1 : 1 + pieces]
    cols = refs[1 + pieces : 1 + pieces + blocks * pieces]
    out, stage, sem = refs[-3:]
    shards, _, rows, _ = own[0].shape
    local = shards * pieces * rows
    width = blocks * local
    lane = lax.broadcasted_iota(jnp.int32, (local, 256), 1)
    at = [pl.ds(pl.multiple_of(place[1 + n] * local, LANES), local) for n in range(blocks)]
    goal = pl.ds(pl.multiple_of(place[0] * width, LANES), width)

    def gather(parts, tile):
        halves = [jnp.stack([part[:, tile + u] for part in parts], axis=1).reshape(local, LANES) for u in range(2)]
        return jnp.concatenate(halves, axis=1)

    def copy(pair):
        return pltpu.make_async_copy(stage.at[pair], out.at[:, pl.ds(2 * pair, 2), :, goal], sem.at[pair])

    for pair in range(CH_DEV // 2):
        q, w = pair // 2, pair % 2
        held = gather(own, 3 * q + w).astype(jnp.float32)
        ahead, behind = pltpu.roll(held, 256 - NSPEC, 1), pltpu.roll(held, NSPEC, 1)
        left = []
        for i in range(2):
            start = w * 64 + i * PAIR
            real = (lane >= start) & (lane < start + NSPEC)
            imag = (lane >= start + NSPEC) & (lane < start + PAIR)
            left.append(jnp.where(real | imag, held, 0.0).astype(jnp.bfloat16))
            left.append(jnp.where(real, ahead, jnp.where(imag, -behind, 0.0)).astype(jnp.bfloat16))
        left = jnp.concatenate(left, axis=0)
        for n in range(blocks):
            right = gather(cols[n * pieces : (n + 1) * pieces], 3 * q + w)
            term = lax.dot_general(left, right, (((1,), (1,)), ((), ())), preferred_element_type=jnp.float32)
            term = (term * (1.0 / NSPEC)).astype(jnp.bfloat16)
            for i in range(2):
                for p in range(2):
                    k = 2 * i + p
                    stage[pair, p, i, :, at[n]] = term[k * local : (k + 1) * local]
        copy(pair).start()
    for pair in range(CH_DEV // 2):
        copy(pair).wait()


def correlate(place, own, cols, parts, before=None):
    pieces = len(own)
    blocks = len(cols) // pieces
    shards, tiles, rows, _ = own[0].shape
    local = shards * pieces * rows
    width = local * blocks
    extra = [] if before is None else [before]
    operands = [place, *own, *cols, *extra]
    here = pl.BlockSpec(memory_space=pltpu.VMEM)
    far = pl.BlockSpec(memory_space=pl.ANY)

    def body(*refs):
        return correlate_kernel(pieces, blocks, *refs[: 1 + pieces + len(cols)], *refs[-3:])

    return pl.pallas_call(
        body,
        in_specs=[pl.BlockSpec(memory_space=pltpu.SMEM)] + [here] * (pieces + len(cols)) + [far] * len(extra),
        out_specs=far,
        out_shape=jax.ShapeDtypeStruct((2, CH_DEV, local, width * parts), jnp.bfloat16),
        scratch_shapes=[
            pltpu.VMEM((CH_DEV // 2, 2, 2, local, width), jnp.bfloat16),
            pltpu.SemaphoreType.DMA((CH_DEV // 2,)),
        ],
        input_output_aliases={len(operands) - 1: 0} if extra else {},
        compiler_params=pltpu.CompilerParams(vmem_limit_bytes=CORRELATE_VMEM),
        cost_estimate=pl.CostEstimate(
            flops=2 * 2 * CH_DEV * local * width * 256, bytes_accessed=2 * 2 * CH_DEV * local * width, transcendentals=0
        ),
        name="correlate",
    )(*operands)


def exchange(value, axis, distance):
    count = lax.axis_size(axis)
    return lax.ppermute(value, axis, [(i, i ^ distance) for i in range(count)])


def per_device(samples):
    antennas, length = samples.shape
    shards = lax.axis_size("freq")
    blocks = lax.axis_size("blk")
    channels = CH_DEV * shards
    frames = length // FRAME
    width = -(-channels // LANES) * LANES
    rows = 16 if antennas % 16 == 0 else 8
    pieces = antennas // rows
    window = jnp.asarray(make_window(FRAME, TAPS))
    table = jnp.asarray(make_table(FRAME, channels, width))
    tiled = samples.reshape(antennas // 8, 8, length // LANES, LANES).transpose(0, 2, 1, 3)
    tiled = tiled.reshape(antennas // 8, frames, FRAME // LANES, 8, LANES)
    own, near, far = [], [], []
    for piece in range(pieces):
        spectra = filterbank(tiled, window, table, piece, rows, shards)
        own.append(lax.all_to_all(spectra, "freq", split_axis=0, concat_axis=0, tiled=True))
        far.append(exchange(own[piece], "blk", 2))
        near.append(exchange(own[piece], "blk", 1))
    me = lax.axis_index("blk")

    def place(n):
        return jnp.stack([(me ^ n) >> 1, me & 1, (me & 1) ^ 1]).astype(jnp.int32)

    last = [exchange(value, "blk", 1) for value in far[:-1]]
    own, near, far[:-1], last = lax.optimization_barrier((own, near, far[:-1], last))
    result = correlate(place(0), own, own + near, blocks // 2)
    result, far[-1] = lax.optimization_barrier((result, far[-1]))
    last.append(exchange(far[-1], "blk", 1))
    return correlate(place(2), own, far + last, blocks // 2, result)


def solution(mesh):
    in_specs = (P(("blk", "freq"), None),)
    out_specs = P(None, "freq", "blk", None)
    return jax.shard_map(
        per_device, mesh=mesh, in_specs=in_specs, out_specs=out_specs, check_vma=False
    )
```

```python
import math

import jax
import jax.numpy as jnp
import ml_dtypes
import numpy as np
from jax import lax
from jax.experimental import pallas as pl
from jax.experimental.pallas import tpu as pltpu
from jax.sharding import PartitionSpec as P

FRAME = 8192
TAPS = 4
CH_DEV = 12
NSPEC = 48
LANES = 128
PAIR = 2 * NSPEC
BLOCK = 2048
PARTS = ((0, 4), (4, 4), (8, 8), (16, 16), (32, 16), (48, 8), (56, 8))
FILTER_VMEM = 60 * 1024 * 1024
CORRELATE_VMEM = 32 * 1024 * 1024


def make_window(frame, taps):
    length = taps * frame
    moment = np.arange(length, dtype=np.float64)
    offset = (moment + 0.5 - length / 2.0) / frame
    taper = 0.5 - 0.5 * np.cos(2.0 * math.pi * (moment + 0.5) / length)
    w = (np.sinc(offset) * taper).astype(np.float32).reshape(taps, frame // LANES, 1, LANES)
    return np.ascontiguousarray(np.broadcast_to(w, (taps, frame // LANES, 8, LANES)))


def make_table(frame, channels, width):
    index = np.arange(frame, dtype=np.int64)[:, None]
    column = np.arange(channels, dtype=np.int64)[None, :] + 1
    phase = (index * column % frame).astype(np.float64) * (2.0 * math.pi / frame)
    factor = 1.0 / math.sqrt(21.25 * frame)
    table = np.zeros((frame, 2 * width), np.float32)
    table[:, :channels] = np.cos(phase) * factor
    table[:, width : width + channels] = -np.sin(phase) * factor
    return table.astype(ml_dtypes.bfloat16)


def filterbank_kernel(piece, rows, channels, width, x_hbm, w_hbm, t_hbm, o_hbm, x_ref, w_ref, t_ref, filt, acc, turned, o_ref, x_sem, w_sem, t_sem, o_sem):
    groups = rows // 8
    spec_rows = NSPEC * rows
    tiles = BLOCK // LANES

    def x_copy(n):
        first, count = PARTS[n]
        where = pl.ds(first, count)
        return pltpu.make_async_copy(
            x_hbm.at[pl.ds(piece * groups, groups), :, where], x_ref.at[:, :, where], x_sem.at[n]
        )

    def t_copy(b):
        return pltpu.make_async_copy(t_hbm.at[pl.ds(b * BLOCK, BLOCK)], t_ref.at[b], t_sem.at[b])

    def o_copy(dest):
        return pltpu.make_async_copy(o_ref.at[dest], o_hbm.at[dest], o_sem.at[dest])

    def w_copy(n):
        where = pl.ds(*PARTS[n])
        return pltpu.make_async_copy(w_hbm.at[:, where], w_ref.at[:, where], w_sem.at[n])

    for n, (first, count) in enumerate(PARTS):
        x_copy(n).start()
        w_copy(n).start()
        if (first + count) % tiles == 0:
            t_copy(first // tiles).start()

    def one_tile(tile, slot):
        taps = [w_ref[k, tile] for k in range(TAPS)]
        held = [[x_ref[g, f, tile].astype(jnp.float32) for f in range(TAPS - 1)] for g in range(groups)]
        ready = []
        for s in range(NSPEC):
            for g in range(groups):
                held[g].append(x_ref[g, s + TAPS - 1, tile].astype(jnp.float32))
                total = held[g][0] * taps[0]
                for k in range(1, TAPS):
                    total = total + held[g][k] * taps[k]
                held[g].pop(0)
                ready.append(total)
                if len(ready) == 2:
                    row = (s * groups + g - 1) * 8
                    filt[slot, pl.ds(row, 16), :] = jnp.concatenate(ready, axis=0).astype(jnp.bfloat16)
                    ready = []

    for n, (first, count) in enumerate(PARTS):
        x_copy(n).wait()
        w_copy(n).wait()
        base = first % tiles

        def step(i, carry, first=first, base=base):
            for u in range(4):
                one_tile(first + 4 * i + u, base + 4 * i + u)
            return carry

        lax.fori_loop(0, count // 4, step, 0)
        if (first + count) % tiles:
            continue
        b = first // tiles
        t_copy(b).wait()
        left = jnp.concatenate([filt[k] for k in range(tiles)], axis=1)
        for m in range(2):
            span = slice(m * spec_rows // 2, (m + 1) * spec_rows // 2)
            part = jnp.dot(left[span], t_ref[b], preferred_element_type=jnp.float32)
            for h in range(2 * width // LANES):
                half = part[:, h * LANES : (h + 1) * LANES]
                if b == 0:
                    acc[h, span] = half
                else:
                    acc[h, span] += half

    for c in range(width // LANES):
        count = min(LANES, channels - c * LANES)
        for a in range(rows):
            both = jnp.concatenate(
                [acc[p * (width // LANES) + c, pl.ds(a, NSPEC, stride=rows), :] for p in range(2)], axis=0
            )
            turned[pl.ds(c * LANES * rows + a, count, stride=rows), pl.ds(0, PAIR)] = both.T[:count]
    lane = lax.broadcasted_iota(jnp.int32, (rows, LANES), 1)
    for q in range(channels // 4):
        one = [turned[pl.ds((4 * q + i) * rows, rows), :] for i in range(4)]
        one = [one[0]] + [pltpu.roll(one[i], LANES - 32 * i, 1) for i in range(1, 4)]
        dest, place = q // (CH_DEV // 4), q % (CH_DEV // 4)
        for i in range(3):
            tile = jnp.where(lane < LANES - 32 * (i + 1), one[i], one[i + 1])
            o_ref[dest, place * 3 + i] = tile.astype(jnp.bfloat16)
        if place == CH_DEV // 4 - 1:
            o_copy(dest).start()
    for dest in range(channels // CH_DEV):
        o_copy(dest).wait()


def filterbank(samples, window, table, piece, rows, shards):
    antenna_groups, frames, _, _, _ = samples.shape
    groups = rows // 8
    channels = CH_DEV * shards
    width = table.shape[1] // 2
    spec_rows = NSPEC * rows
    shape = (shards, CH_DEV * PAIR // LANES, rows, LANES)
    return pl.pallas_call(
        lambda *refs: filterbank_kernel(piece, rows, channels, width, *refs),
        in_specs=[
            pl.BlockSpec(memory_space=pl.ANY),
            pl.BlockSpec(memory_space=pl.ANY),
            pl.BlockSpec(memory_space=pl.ANY),
        ],
        out_specs=pl.BlockSpec(memory_space=pl.ANY),
        out_shape=jax.ShapeDtypeStruct(shape, jnp.bfloat16),
        scratch_shapes=[
            pltpu.VMEM((groups, frames, FRAME // LANES, 8, LANES), jnp.int32),
            pltpu.VMEM((TAPS, FRAME // LANES, 8, LANES), jnp.float32),
            pltpu.VMEM((FRAME // BLOCK, BLOCK, 2 * width), jnp.bfloat16),
            pltpu.VMEM((BLOCK // LANES, spec_rows, LANES), jnp.bfloat16),
            pltpu.VMEM((2 * width // LANES, spec_rows, LANES), jnp.float32),
            pltpu.VMEM((channels * rows, LANES), jnp.float32),
            pltpu.VMEM(shape, jnp.bfloat16),
            pltpu.SemaphoreType.DMA((len(PARTS),)),
            pltpu.SemaphoreType.DMA((len(PARTS),)),
            pltpu.SemaphoreType.DMA((FRAME // BLOCK,)),
            pltpu.SemaphoreType.DMA((shards,)),
        ],
        compiler_params=pltpu.CompilerParams(vmem_limit_bytes=FILTER_VMEM),
        cost_estimate=pl.CostEstimate(
            flops=2 * spec_rows * FRAME * 2 * width, bytes_accessed=4 * rows * frames * FRAME, transcendentals=0
        ),
        name="filterbank",
    )(samples, window, table)


def correlate_kernel(pieces, blocks, *refs):
    place, own = refs[0], refs[1 : 1 + pieces]
    cols = refs[1 + pieces : 1 + pieces + blocks * pieces]
    out, stage, sem = refs[-3:]
    shards, _, rows, _ = own[0].shape
    local = shards * pieces * rows
    width = blocks * local
    lane = lax.broadcasted_iota(jnp.int32, (local, 256), 1)
    at = [pl.ds(pl.multiple_of(place[1 + n] * local, LANES), local) for n in range(blocks)]
    goal = pl.ds(pl.multiple_of(place[0] * width, LANES), width)

    def gather(parts, tile):
        halves = [jnp.stack([part[:, tile + u] for part in parts], axis=1).reshape(local, LANES) for u in range(2)]
        return jnp.concatenate(halves, axis=1)

    def copy(pair):
        return pltpu.make_async_copy(stage.at[pair], out.at[:, pl.ds(2 * pair, 2), :, goal], sem.at[pair])

    for pair in range(CH_DEV // 2):
        q, w = pair // 2, pair % 2
        held = gather(own, 3 * q + w).astype(jnp.float32)
        ahead, behind = pltpu.roll(held, 256 - NSPEC, 1), pltpu.roll(held, NSPEC, 1)
        left = []
        for i in range(2):
            start = w * 64 + i * PAIR
            real = (lane >= start) & (lane < start + NSPEC)
            imag = (lane >= start + NSPEC) & (lane < start + PAIR)
            left.append(jnp.where(real | imag, held, 0.0).astype(jnp.bfloat16))
            left.append(jnp.where(real, ahead, jnp.where(imag, -behind, 0.0)).astype(jnp.bfloat16))
        for n in range(blocks):
            right = gather(cols[n * pieces : (n + 1) * pieces], 3 * q + w)
            for i in range(2):
                for p in range(2):
                    term = lax.dot_general(
                        left[2 * i + p], right, (((1,), (1,)), ((), ())), preferred_element_type=jnp.float32
                    )
                    stage[pair, p, i, :, at[n]] = (term * (1.0 / NSPEC)).astype(jnp.bfloat16)
        copy(pair).start()
    for pair in range(CH_DEV // 2):
        copy(pair).wait()


def correlate(place, own, cols, parts, before=None):
    pieces = len(own)
    blocks = len(cols) // pieces
    shards, tiles, rows, _ = own[0].shape
    local = shards * pieces * rows
    width = local * blocks
    extra = [] if before is None else [before]
    operands = [place, *own, *cols, *extra]
    here = pl.BlockSpec(memory_space=pltpu.VMEM)
    far = pl.BlockSpec(memory_space=pl.ANY)

    def body(*refs):
        return correlate_kernel(pieces, blocks, *refs[: 1 + pieces + len(cols)], *refs[-3:])

    return pl.pallas_call(
        body,
        in_specs=[pl.BlockSpec(memory_space=pltpu.SMEM)] + [here] * (pieces + len(cols)) + [far] * len(extra),
        out_specs=far,
        out_shape=jax.ShapeDtypeStruct((2, CH_DEV, local, width * parts), jnp.bfloat16),
        scratch_shapes=[
            pltpu.VMEM((CH_DEV // 2, 2, 2, local, width), jnp.bfloat16),
            pltpu.SemaphoreType.DMA((CH_DEV // 2,)),
        ],
        input_output_aliases={len(operands) - 1: 0} if extra else {},
        compiler_params=pltpu.CompilerParams(vmem_limit_bytes=CORRELATE_VMEM),
        cost_estimate=pl.CostEstimate(
            flops=2 * 2 * CH_DEV * local * width * 256, bytes_accessed=2 * 2 * CH_DEV * local * width, transcendentals=0
        ),
        name="correlate",
    )(*operands)


def exchange(value, axis, distance):
    count = lax.axis_size(axis)
    return lax.ppermute(value, axis, [(i, i ^ distance) for i in range(count)])


def per_device(samples):
    antennas, length = samples.shape
    shards = lax.axis_size("freq")
    blocks = lax.axis_size("blk")
    channels = CH_DEV * shards
    frames = length // FRAME
    width = -(-channels // LANES) * LANES
    rows = 16 if antennas % 16 == 0 else 8
    pieces = antennas // rows
    window = jnp.asarray(make_window(FRAME, TAPS))
    table = jnp.asarray(make_table(FRAME, channels, width))
    tiled = samples.reshape(antennas // 8, 8, length // LANES, LANES).transpose(0, 2, 1, 3)
    tiled = tiled.reshape(antennas // 8, frames, FRAME // LANES, 8, LANES)
    own, near, far = [], [], []
    for piece in range(pieces):
        spectra = filterbank(tiled, window, table, piece, rows, shards)
        own.append(lax.all_to_all(spectra, "freq", split_axis=0, concat_axis=0, tiled=True))
        far.append(exchange(own[piece], "blk", 2))
        near.append(exchange(own[piece], "blk", 1))
    me = lax.axis_index("blk")

    def place(n):
        return jnp.stack([(me ^ n) >> 1, me & 1, (me & 1) ^ 1]).astype(jnp.int32)

    last = [exchange(value, "blk", 1) for value in far[:-1]]
    own, near, far[:-1], last = lax.optimization_barrier((own, near, far[:-1], last))
    result = correlate(place(0), own, own + near, blocks // 2)
    result, far[-1] = lax.optimization_barrier((result, far[-1]))
    last.append(exchange(far[-1], "blk", 1))
    return correlate(place(2), own, far + last, blocks // 2, result)


def solution(mesh):
    in_specs = (P(("blk", "freq"), None),)
    out_specs = P(None, "freq", "blk", None)
    return jax.shard_map(
        per_device, mesh=mesh, in_specs=in_specs, out_specs=out_specs, check_vma=False
    )
```
